32 devices in a mesh: dp: 4 (over z), section: 4 (over x, core), mp: 2 (over y).
Axes of the slice: x: 2, y: 2, z: 4, core: 2. Of those that a mesh axis runs over, the one named last changes fastest.
Arguments:
- arriving: bfloat16 [4, 576, 8192], P('section', 'dp', 'mp'), may hold values from -6 to 6
- keep_mask: int32 [576], P('dp'), may hold values 0 or 1
- mask_vector: bfloat16 [8192], P('mp'), may hold values from -5 to 5
- stashed: bfloat16 [4, 576, 8192], P('section', 'dp', 'mp'), may hold values from -6 to 6
- cotangent: bfloat16 [4, 576, 8192], P('section', 'dp', 'mp'), may hold values from -6 to 6
- gain: bfloat16 [4, 8192], P('section', 'mp'), may hold values from 0.3984375 to 1.59375
- down_adapter: bfloat16 [4, 8192, 256], P('section', None, 'mp'), may hold values from -0.0625 to 0.0625
- up_adapter: bfloat16 [4, 256, 8192], P('section', 'mp'), may hold values from -0.375 to 0.375
Outputs:
- next_input: bfloat16 [4, 576, 8192], P('section', 'dp', 'mp')
- prev_grad: bfloat16 [4, 576, 8192], P('section', 'dp', 'mp')
- down_grad: float32 [4, 8192, 256], P('section', 'dp', 'mp')
- up_grad: float32 [4, 256, 8192], P('section', 'mp', 'dp')
The draws below stay inside these ranges and needn't reach their ends.
All inputs are finite; a program needn't handle non-finite values. No bound on the sum of `keep_mask` on one device may be relied on, other than what follows from the above.
Results may differ from the reference program's by a relative error of at most 0.0015.
The reference program's roundings to bfloat16 on the way count: a program that leaves them out, or rounds other values in their place, can miss the bound.
Values may be sent and summed in bfloat16 or wider, within the bound.
A program may use at most 128 MiB of HBM per device.

```python
import jax
import jax.numpy as jnp
from jax import lax

D = 8192
R = 256
TOKENS = 576
SECTIONS = 4
N_DP = 4


def place_ends(entries, stream_key, smallest, top_value):
    shape = entries.shape
    index_at = [jax.random.randint(jax.random.fold_in(stream_key, axis), (), 0, shape[axis]) for axis in range(len(shape))]
    entries = entries.at[tuple(index_at)].set(smallest)
    longest = shape.index(max(shape))
    index_at[longest] = (index_at[longest] + 1) % shape[longest]
    return entries.at[tuple(index_at)].set(top_value)


def raised(drawn, own_key, source, target, blocks, factor):
    def block_of(axis_at):
        return (jnp.arange(drawn.shape[axis_at]) // (drawn.shape[axis_at] // blocks)).reshape((-1,) + (1,) * (drawn.ndim - 1 - axis_at))

    near = jax.random.permutation(own_key, blocks)[block_of(target)]
    far = (block_of(target) + blocks // 2) % blocks
    return jnp.where((block_of(source) == near) | (block_of(source) == far), factor * drawn, drawn)


def block_scale(own_key, dims, pieces, smallest, largest):
    def one(dim, blocks):
        draws = jax.random.uniform(jax.random.fold_in(jax.random.fold_in(own_key, 6), dim), (blocks,), jnp.float32, smallest / len(pieces), largest / len(pieces))
        return jnp.repeat(jnp.exp(draws), dims[dim] // blocks).reshape((-1,) + (1,) * (len(dims) - dim - 1))

    level = one(*pieces[0])
    for cut in pieces[1:]:
        level = level * one(*cut)
    return level


def noise(own_key, shape, deviation, limit, cuts=(), kind=jnp.bfloat16):
    level = block_scale(own_key, shape, cuts, -0.22, 0.18) if cuts else 1.0
    entries = jax.random.normal(own_key, shape, jnp.float32) * deviation * level
    return jnp.minimum(jnp.maximum(entries, -limit), limit).astype(kind)


def noise_with(own_key, shape, scale, limit, cuts, heavy, held_as=jnp.bfloat16):
    drawn = scale * jax.random.normal(own_key, shape, jnp.float32)
    if cuts:
        drawn = drawn * block_scale(own_key, shape, cuts, -0.22, 0.18)
    return jnp.clip(raised(drawn, jax.random.fold_in(own_key, 3), *heavy), -limit, limit).astype(held_as)


def setup_inputs(seed: int = 0) -> dict:
    splits = jax.random.split(jax.random.key(seed), 9)
    arriving = noise(splits[0], (SECTIONS, TOKENS, D), 1.0, 6.0, ((0, 4), (1, 4), (2, 2)))
    keep_mask = place_ends((jax.random.randint(splits[1], (TOKENS,), 0, 10) < 3).astype(jnp.int32), jax.random.fold_in(splits[1], 1), 0, 1)
    mask_vector = noise(splits[2], (D,), 1.0, 5.0, ((0, 2),))
    stashed = noise_with(splits[3], (SECTIONS, TOKENS, D), 1.0, 6.0, ((0, 4), (1, 4), (2, 2)), (1, 2, 4, 2.0))
    cotangent = noise_with(splits[4], (SECTIONS, TOKENS, D), 1.0, 6.0, ((0, 4), (1, 4), (2, 2)), (1, 2, 4, 2.0))
    gain = jnp.clip(1.0 + 0.12 * jax.random.normal(splits[5], (SECTIONS, D), jnp.float32), 0.3984375, 1.59375).astype(jnp.bfloat16)
    down_adapter = noise(splits[6], (SECTIONS, D, R), D ** -0.5, 0.0625, ((0, 4), (2, 2)))
    up_adapter = noise(splits[7], (SECTIONS, R, D), R ** -0.5, 0.375, ((0, 4), (1, 2)))
    return dict(arriving=arriving, keep_mask=keep_mask, mask_vector=mask_vector, stashed=stashed, cotangent=cotangent, gain=gain, down_adapter=down_adapter, up_adapter=up_adapter)


def row_scale(rows):
    values = rows.astype(jnp.float32)
    return lax.rsqrt(lax.optimization_barrier(jnp.mean(values * values, axis=1, keepdims=True)) + 1e-05)

def contract_rows(left, right):
    return lax.dot_general(left, right, (((0,), (0,)), ((), ())), preferred_element_type=jnp.float32)

def contract_cols(left, right):
    return lax.dot_general(left, right, (((1,), (1,)), ((), ())), preferred_element_type=jnp.float32)

def reference(arriving, keep_mask, mask_vector, stashed, cotangent, gain, down_adapter, up_adapter):
    outputs = []
    backs = []
    down_grads = []
    up_grads = []
    for position in range(SECTIONS):
        gain_row = gain[position].astype(jnp.float32)[None, :]
        inputs = arriving[position]
        if position == 0:
            inputs = jnp.where(keep_mask[:, None] == 1, inputs, mask_vector[None, :])
        normed = (inputs.astype(jnp.float32) * row_scale(inputs) * gain_row).astype(jnp.bfloat16)
        hidden_pre = jnp.dot(normed, down_adapter[position], preferred_element_type=jnp.float32)
        hidden = jax.nn.silu(hidden_pre).astype(jnp.bfloat16)
        branch = jnp.dot(hidden, up_adapter[position], preferred_element_type=jnp.float32)
        outputs.append((inputs.astype(jnp.float32) + branch).astype(jnp.bfloat16))
        saved = stashed[position]
        upstream = cotangent[position]
        saved_scale = row_scale(saved)
        saved_values = saved.astype(jnp.float32)
        saved_normed = (saved_values * saved_scale * gain_row).astype(jnp.bfloat16)
        saved_pre = jnp.dot(saved_normed, down_adapter[position], preferred_element_type=jnp.float32)
        sigmoid_pre = jax.nn.sigmoid(saved_pre)
        saved_hidden = (saved_pre * sigmoid_pre).astype(jnp.bfloat16)
        hidden_grad = contract_cols(upstream, up_adapter[position])
        pre_grad = (hidden_grad * sigmoid_pre * (1.0 + saved_pre * (1.0 - sigmoid_pre))).astype(jnp.bfloat16)
        normed_grad = contract_cols(pre_grad, down_adapter[position])
        scaled_grad = normed_grad * gain_row
        row_dot = lax.optimization_barrier(jnp.sum(saved_values * scaled_grad, axis=1, keepdims=True))
        cubed = saved_scale * saved_scale * saved_scale
        input_grad = upstream.astype(jnp.float32) + saved_scale * scaled_grad - saved_values * cubed * (row_dot / D)
        backs.append(input_grad.astype(jnp.bfloat16))
        down_grads.append(contract_rows(saved_normed, pre_grad) / N_DP)
        up_grads.append(contract_rows(saved_hidden, upstream) / N_DP)
    zeros = jnp.zeros_like(arriving[0])
    next_input = jnp.stack([zeros] + outputs[:-1])
    prev_grad = jnp.stack(backs[1:] + [zeros])
    return (next_input, prev_grad, jnp.stack(down_grads), jnp.stack(up_grads))
```

```python
import functools

import jax
import jax.numpy as jnp
from jax import lax
from jax.experimental import pallas as pl
from jax.experimental.pallas import tpu as pltpu
from jax.sharding import PartitionSpec as P

F32 = jnp.float32
BF16 = jnp.bfloat16
MESH = pl.DeviceIdType.MESH


def dot(left, right, dims):
    return lax.dot_general(left, right, (dims, ((), ())), preferred_element_type=F32)


def kernel(
    sizes,
    arr, keep, maskv, sta, cot, gain, down, up,
    nxt, prv, dgo, ugo,
    wd, wu, xin, normed, scaled, acts, pg, sc_all, nall,
    ss_loc, ss_rem, g_own, g_rem, part, part_rem, rd_loc, rd_rem, out_st, grad_st, res_d, res_u,
    w_ssem, w_rsem, w_lsem, g_ssem, g_rsem, ss_ssem, ss_rsem, a_ssem, a_rsem, a_lsem,
    p_ssem, p_rsem, pg_ssem, pg_rsem, sc_ssem, sc_rsem, rd_ssem, rd_rsem,
    o_ssem, o_rsem, r_ssem, r_rsem,
):
    Z, S, rows, half, units = sizes
    H = Z // 2
    full = 2 * half
    F = full // (2 * Z)
    C = min(half, 512)
    chunks = half // C
    d = lax.axis_index("dp")
    s = lax.axis_index("section")
    m = lax.axis_index("mp")
    om = 1 - m
    peer = (d, s, om)

    def rcopy(src, dst, ssem, rsem, dev):
        return pltpu.make_async_remote_copy(
            src_ref=src, dst_ref=dst, send_sem=ssem, recv_sem=rsem,
            device_id=dev, device_id_type=MESH,
        )

    barrier = pltpu.get_barrier_semaphore()

    @pl.loop(0, Z)
    def _(i):
        pl.semaphore_signal(barrier, inc=1, device_id=(i, s, om), device_id_type=MESH)

    @pl.loop(1, Z)
    def _(i):
        pl.semaphore_signal(
            barrier, inc=1, device_id=(lax.rem(d + i, Z), s, m), device_id_type=MESH
        )

    @pl.when(s > 0)
    def _():
        pl.semaphore_signal(barrier, inc=1, device_id=(d, s - 1, m), device_id_type=MESH)

    @pl.when(s < S - 1)
    def _():
        pl.semaphore_signal(barrier, inc=1, device_id=(d, s + 1, m), device_id_type=MESH)

    @pl.when(jnp.logical_and(s > 0, s < S - 1))
    def _():
        pl.semaphore_wait(barrier, 2 * Z + 1)

    @pl.when(jnp.logical_or(s == 0, s == S - 1))
    def _():
        pl.semaphore_wait(barrier, 2 * Z)

    mine = pl.multiple_of(m * half, half)
    other = pl.multiple_of(om * half, half)
    send_up = rcopy(up.at[:, pl.ds(other, half)], wu.at[pl.ds(units, units), :],
                    w_ssem.at[0], w_rsem.at[0], peer)
    send_down = rcopy(down.at[pl.ds(other, half), :], wd.at[:, pl.ds(units, units)],
                      w_ssem.at[1], w_rsem.at[1], peer)
    send_up.start()
    send_down.start()
    own_up = pltpu.make_async_copy(up.at[:, pl.ds(mine, half)], wu.at[pl.ds(0, units), :], w_lsem.at[0])
    own_down = pltpu.make_async_copy(down.at[pl.ds(mine, half), :], wd.at[:, pl.ds(0, units)], w_lsem.at[1])
    own_up.start()
    own_down.start()

    def act_copy(a, src, j, mt):
        col = pl.multiple_of((j * 2 + mt) * F, F)
        to = m * H + j
        return rcopy(src.at[:, pl.ds(col, F)], acts.at[a, d], a_ssem.at[a, j * 2 + mt],
                     a_rsem.at[a, d], (to, s, mt))

    def act_own(a, src):
        col = pl.multiple_of(((d - m * H) * 2 + m) * F, F)
        return pltpu.make_async_copy(src.at[:, pl.ds(col, F)], acts.at[a, d], a_lsem.at[a])

    keeps_own = (d // H) == m

    def plane_sends(go, a, src):
        @pl.loop(0, H)
        def _(j):
            @pl.when(m * H + j != d)
            def _():
                go(act_copy(a, src, j, m))

    def cross_sends(go, a, src):
        @pl.loop(0, H)
        def _(j):
            go(act_copy(a, src, j, om))

    for a, src in ((0, sta), (1, cot)):
        plane_sends(lambda c: c.start(), a, src)

        @pl.when(keeps_own)
        def _():
            act_own(a, src).start()

    g_own[...] = gain[...].astype(F32)
    gain_copy = rcopy(g_own, g_rem, g_ssem, g_rsem, peer)
    gain_copy.start()

    keep_row = jnp.logical_or(keep[...] == 1, s != 0)

    def at(i, size=C):
        return pl.ds(pl.multiple_of(i * size, size), size)

    def fold(v):
        total = v[:, :128]
        for k in range(1, v.shape[1] // 128):
            total = total + v[:, 128 * k:128 * (k + 1)]
        return total

    def squares(i, carry):
        cx, cs = carry
        v = jnp.where(keep_row, arr[:, at(i)].astype(F32), maskv[:, at(i)].astype(F32))
        xin[:, at(i)] = v.astype(BF16)
        w = sta[:, at(i)].astype(F32)
        return cx + fold(v * v), cs + fold(w * w)

    zero = jnp.zeros((rows, 128), F32)
    cx, cs = lax.fori_loop(0, chunks, squares, (zero, zero))
    lane = lax.broadcasted_iota(jnp.int32, (rows, 128), 1)
    ss_loc[...] = jnp.where(
        lane < 64, jnp.sum(cx, axis=1, keepdims=True), jnp.sum(cs, axis=1, keepdims=True)
    )
    ss_copy = rcopy(ss_loc, ss_rem, ss_ssem, ss_rsem, peer)
    ss_copy.start()

    def part_copy(k):
        return rcopy(part.at[k], part_rem.at[k], p_ssem.at[k], p_rsem.at[k], peer)

    acc0 = jnp.zeros((rows, 2 * units), F32)
    own_up.wait()
    send_up.wait_recv()
    part[0] = lax.fori_loop(
        0, chunks, lambda i, acc: acc + dot(cot[:, at(i)], wu[:, at(i)], ((1,), (1,))), acc0
    )
    part_copy(0).start()

    ss_copy.wait_recv()
    total = (ss_loc[...] + ss_rem[...]) / full
    scales = lax.rsqrt(total + 1e-05)
    scale_f = scales[:, 0:1]
    scale_b = scales[:, 127:128]
    sc_all[d] = jnp.broadcast_to(scale_b, (rows, 128))

    def sc_copy(i):
        return rcopy(sc_all.at[d], sc_all.at[d], sc_ssem.at[i], sc_rsem.at[d],
                     (lax.rem(d + i, Z), s, m))

    @pl.loop(1, Z)
    def _(i):
        sc_copy(i).start()

    def normalise(k, src, scale):
        @pl.loop(0, chunks)
        def _(i):
            normed[k, :, at(i)] = (
                src[:, at(i)].astype(F32) * scale * g_own[:, at(i)]
            ).astype(BF16)

    normalise(0, sta, scale_b)
    normalise(1, xin, scale_f)
    own_down.wait()
    send_down.wait_recv()
    for k in (0, 1):
        part[1 + k] = lax.fori_loop(
            0, chunks, lambda i, acc: acc + dot(normed[k, :, at(i)], wd[at(i), :], ((1,), (0,))), acc0
        )
        part_copy(1 + k).start()

    send_up.wait_send()
    send_down.wait_send()
    for a, src in ((0, sta), (1, cot)):
        cross_sends(lambda c: c.start(), a, src)

    def whole_sum(k):
        part_copy(k).wait_recv()
        return jnp.concatenate(
            [part[k, :, :units] + part_rem[k, :, units:], part[k, :, units:] + part_rem[k, :, :units]],
            axis=1,
        )

    hidden_grad = whole_sum(0)
    saved_pre = whole_sum(1)
    sigma = jax.nn.sigmoid(saved_pre)
    pre_grad = (hidden_grad * sigma * (1.0 + saved_pre * (1.0 - sigma))).astype(BF16)
    pg[d, :, :2 * units] = pre_grad
    pg[d, :, 2 * units:] = (saved_pre * sigma).astype(BF16)

    def pg_copy(i):
        return rcopy(pg.at[d], pg.at[d], pg_ssem.at[i], pg_rsem.at[d],
                     (lax.rem(d + i, Z), s, m))

    @pl.loop(1, Z)
    def _(i):
        pg_copy(i).start()

    def grads(i, acc):
        v = dot(pre_grad, wd[at(i), :], ((1,), (1,))) * g_own[:, at(i)]
        scaled[:, at(i)] = v
        return acc + fold(v * sta[:, at(i)].astype(F32))

    rdot = lax.fori_loop(0, chunks, grads, zero)
    rd_loc[...] = jnp.broadcast_to(jnp.sum(rdot, axis=1, keepdims=True), (rows, 128))
    rd_copy = rcopy(rd_loc, rd_rem, rd_ssem, rd_rsem, peer)
    rd_copy.start()

    pre = whole_sum(2)
    hidden = (pre * jax.nn.sigmoid(pre)).astype(BF16)

    @pl.loop(0, chunks)
    def _(i):
        out_st[:, at(i)] = (
            xin[:, at(i)].astype(F32) + dot(hidden, wu[:, at(i)], ((1,), (0,)))
        ).astype(BF16)

    def out_copy():
        return rcopy(out_st, nxt, o_ssem.at[0], o_rsem.at[0], (d, s + 1, m))

    def grad_copy():
        return rcopy(grad_st, prv, o_ssem.at[1], o_rsem.at[1], (d, s - 1, m))

    @pl.when(s < S - 1)
    def _():
        out_copy().start()

    rd_copy.wait_recv()
    row_dot = (rd_loc[...] + rd_rem[...])[:, 0:1]
    back = scale_b * scale_b * scale_b * (row_dot / full)

    @pl.loop(0, chunks)
    def _(i):
        grad_st[:, at(i)] = (
            cot[:, at(i)].astype(F32) + scale_b * scaled[:, at(i)] - sta[:, at(i)].astype(F32) * back
        ).astype(BF16)

    @pl.when(s > 0)
    def _():
        grad_copy().start()

    @pl.when(s == 0)
    def _():
        nxt[...] = jnp.zeros_like(nxt)

    @pl.when(s == S - 1)
    def _():
        prv[...] = jnp.zeros_like(prv)

    gain_copy.wait_recv()
    FC = min(F, 512)
    slice_half = d // H
    gcol = pl.multiple_of(((d - slice_half * H) * 2 + m) * F, F)

    def wait_act(a, i):
        local = jnp.logical_and(i == d, keeps_own)

        @pl.when(local)
        def _():
            act_own(a, sta if a == 0 else cot).wait()

        @pl.when(jnp.logical_not(local))
        def _():
            rcopy(acts.at[a, i], acts.at[a, i], a_ssem.at[a, 0], a_rsem.at[a, i], peer).wait_recv()

    @pl.loop(0, Z)
    def _(i):
        wait_act(1, i)

        @pl.when(i != d)
        def _():
            rcopy(pg.at[i], pg.at[i], pg_ssem.at[0], pg_rsem.at[i], peer).wait_recv()
            rcopy(sc_all.at[i], sc_all.at[i], sc_ssem.at[0], sc_rsem.at[i], peer).wait_recv()

    def res_copy(k):
        if k == 0:
            return rcopy(res_u, ugo.at[:, pl.ds(pl.multiple_of(m * F, F), F)],
                         r_ssem.at[0], r_rsem.at[0], peer)
        return rcopy(res_d, dgo.at[pl.ds(pl.multiple_of(m * F, F), F), :],
                     r_ssem.at[1], r_rsem.at[1], peer)

    tokens = Z * rows
    hid_all = pg[:, :, 2 * units:].reshape(tokens, 2 * units)
    for c in range(F // FC):
        cols = slice(c * FC, (c + 1) * FC)
        got = dot(hid_all, acts[1, :, :, cols].reshape(tokens, FC), ((0,), (0,))) / Z
        ugo[:, pl.ds(pl.multiple_of(m * F + c * FC, FC), FC)] = got[:units]
        res_u[:, cols] = got[units:]
    res_copy(0).start()

    @pl.loop(0, Z)
    def _(i):
        wait_act(0, i)
        g = jnp.where(slice_half == m, g_own[:, pl.ds(gcol, F)], g_rem[:, pl.ds(gcol, F)])
        nall[i] = (acts[0, i].astype(F32) * sc_all[i][:, 0:1] * g).astype(BF16)

    pg_all = pg[:, :, :2 * units].reshape(tokens, 2 * units)
    for c in range(F // FC):
        cols = slice(c * FC, (c + 1) * FC)
        got = dot(nall[:, :, cols].reshape(tokens, FC), pg_all, ((0,), (0,))) / Z
        dgo[pl.ds(pl.multiple_of(m * F + c * FC, FC), FC), :] = got[:, :units]
        res_d[cols, :] = got[:, units:]
    res_copy(1).start()

    for a, src in ((0, sta), (1, cot)):
        plane_sends(lambda c: c.wait_send(), a, src)
        cross_sends(lambda c: c.wait_send(), a, src)
    gain_copy.wait_send()
    ss_copy.wait_send()
    rd_copy.wait_send()
    for k in range(3):
        part_copy(k).wait_send()

    @pl.loop(1, Z)
    def _(i):
        sc_copy(i).wait_send()
        pg_copy(i).wait_send()

    @pl.when(s < S - 1)
    def _():
        out_copy().wait_send()
        grad_copy().wait_recv()

    @pl.when(s > 0)
    def _():
        out_copy().wait_recv()
        grad_copy().wait_send()

    res_copy(0).wait()
    res_copy(1).wait()


def on_device(Z, S, arriving, keep_mask, mask_vector, stashed, cotangent, gain, down_adapter, up_adapter):
    _, rows, half = arriving.shape
    units = up_adapter.shape[1]
    F = half // Z
    full = 2 * half
    vm = pl.BlockSpec(memory_space=pltpu.VMEM)
    hbm = pl.BlockSpec(memory_space=pl.ANY)
    dma = pltpu.SemaphoreType.DMA
    vmem = pltpu.VMEM
    nxt, prv, dgo, ugo = pl.pallas_call(
        functools.partial(kernel, (Z, S, rows, half, units)),
        out_shape=(
            jax.ShapeDtypeStruct((rows, half), BF16),
            jax.ShapeDtypeStruct((rows, half), BF16),
            jax.ShapeDtypeStruct((full // Z, units), F32),
            jax.ShapeDtypeStruct((units, full // Z), F32),
        ),
        in_specs=[vm] * 6 + [hbm] * 2,
        out_specs=(vm,) * 4,
        scratch_shapes=[
            vmem((half, 2 * units), BF16),
            vmem((2 * units, half), BF16),
            vmem((rows, half), BF16),
            vmem((2, rows, half), BF16),
            vmem((rows, half), F32),
            vmem((2, Z, rows, F), BF16),
            vmem((Z, rows, 4 * units), BF16),
            vmem((Z, rows, 128), F32),
            vmem((Z, rows, F), BF16),
            vmem((rows, 128), F32),
            vmem((rows, 128), F32),
            vmem((1, half), F32),
            vmem((1, half), F32),
            vmem((3, rows, 2 * units), F32),
            vmem((3, rows, 2 * units), F32),
            vmem((rows, 128), F32),
            vmem((rows, 128), F32),
            vmem((rows, half), BF16),
            vmem((rows, half), BF16),
            vmem((F, units), F32),
            vmem((units, F), F32),
            dma((2,)), dma((2,)), dma((2,)), dma, dma, dma, dma,
            dma((2, Z)), dma((2, Z)), dma((2,)),
            dma((3,)), dma((3,)), dma((Z,)), dma((Z,)), dma((Z,)), dma((Z,)), dma, dma,
            dma((2,)), dma((2,)), dma((2,)), dma((2,)),
        ],
        compiler_params=pltpu.CompilerParams(
            collective_id=0, has_side_effects=True, vmem_limit_bytes=56 * 1024 * 1024
        ),
    )(
        arriving[0], keep_mask[:, None], mask_vector[None], stashed[0], cotangent[0],
        gain, down_adapter[0], up_adapter[0],
    )
    return nxt[None], prv[None], dgo[None], ugo[None]


def solution(mesh):
    return jax.shard_map(
        functools.partial(on_device, mesh.shape["dp"], mesh.shape["section"]),
        mesh=mesh,
        in_specs=(
            P("section", "dp", "mp"),
            P("dp"),
            P("mp"),
            P("section", "dp", "mp"),
            P("section", "dp", "mp"),
            P("section", "mp"),
            P("section", None, "mp"),
            P("section", "mp", None),
        ),
        out_specs=(
            P("section", "dp", "mp"),
            P("section", "dp", "mp"),
            P("section", "dp", "mp"),
            P("section", "mp", "dp"),
        ),
        check_vma=False,
    )
```

```python
import functools

import jax
import jax.numpy as jnp
from jax import lax
from jax.experimental import pallas as pl
from jax.experimental.pallas import tpu as pltpu
from jax.sharding import PartitionSpec as P

F32 = jnp.float32
BF16 = jnp.bfloat16
MESH = pl.DeviceIdType.MESH


def dot(left, right, dims):
    return lax.dot_general(left, right, (dims, ((), ())), preferred_element_type=F32)


def kernel(
    sizes,
    arr, keep, maskv, sta, cot, gain, down, up,
    nxt, prv, dgo, ugo,
    wd, wu, xin, normed, scaled, acts, pg, sc_all, nall,
    ss_loc, ss_rem, g_own, g_rem, part, part_rem, rd_loc, rd_rem, out_st, grad_st, res_d, res_u, rem_d, rem_u, xb,
    w_ssem, w_rsem, w_lsem, g_ssem, g_rsem, ss_ssem, ss_rsem, a_ssem, a_rsem, a_lsem, x_ssem, x_rsem,
    p_ssem, p_rsem, pg_ssem, pg_rsem, sc_ssem, sc_rsem, rd_ssem, rd_rsem,
    o_ssem, o_rsem, r_ssem, r_rsem,
):
    Z, S, rows, half, units = sizes
    H = Z // 2
    full = 2 * half
    F = full // (2 * Z)
    C = min(half, 512)
    chunks = half // C
    d = lax.axis_index("dp")
    s = lax.axis_index("section")
    m = lax.axis_index("mp")
    om = 1 - m
    peer = (d, s, om)

    def rcopy(src, dst, ssem, rsem, dev):
        return pltpu.make_async_remote_copy(
            src_ref=src, dst_ref=dst, send_sem=ssem, recv_sem=rsem,
            device_id=dev, device_id_type=MESH,
        )

    barrier = pltpu.get_barrier_semaphore()

    @pl.loop(0, Z)
    def _(i):
        pl.semaphore_signal(barrier, inc=1, device_id=(i, s, om), device_id_type=MESH)

    @pl.loop(1, Z)
    def _(i):
        pl.semaphore_signal(
            barrier, inc=1, device_id=(lax.rem(d + i, Z), s, m), device_id_type=MESH
        )

    @pl.when(s > 0)
    def _():
        pl.semaphore_signal(barrier, inc=1, device_id=(d, s - 1, m), device_id_type=MESH)

    @pl.when(s < S - 1)
    def _():
        pl.semaphore_signal(barrier, inc=1, device_id=(d, s + 1, m), device_id_type=MESH)

    @pl.when(jnp.logical_and(s > 0, s < S - 1))
    def _():
        pl.semaphore_wait(barrier, 2 * Z + 1)

    @pl.when(jnp.logical_or(s == 0, s == S - 1))
    def _():
        pl.semaphore_wait(barrier, 2 * Z)

    mine = pl.multiple_of(m * half, half)
    other = pl.multiple_of(om * half, half)
    send_up = rcopy(up.at[:, pl.ds(other, half)], wu.at[pl.ds(units, units), :],
                    w_ssem.at[0], w_rsem.at[0], peer)
    send_down = rcopy(down.at[pl.ds(other, half), :], wd.at[:, pl.ds(units, units)],
                      w_ssem.at[1], w_rsem.at[1], peer)
    own_up = pltpu.make_async_copy(up.at[:, pl.ds(mine, half)], wu.at[pl.ds(0, units), :], w_lsem.at[0])
    own_down = pltpu.make_async_copy(down.at[pl.ds(mine, half), :], wd.at[:, pl.ds(0, units)], w_lsem.at[1])
    own_up.start()
    own_down.start()

    def act_copy(a, src, j):
        col = pl.multiple_of((j * 2 + m) * F, F)
        return rcopy(src.at[:, pl.ds(col, F)], acts.at[a, d], a_ssem.at[a, j],
                     a_rsem.at[a, d], (m * H + j, s, m))

    def cross_copy(a, src, j):
        col = pl.multiple_of((j * 2 + om) * F, F)
        return rcopy(src.at[:, pl.ds(col, F)], xb.at[a, j], x_ssem.at[a, j], x_rsem.at[a, j], peer)

    def pass_on(a, j):
        return rcopy(xb.at[a, j], acts.at[a, d], a_ssem.at[a, H + j],
                     a_rsem.at[a, d], (om * H + j, s, m))

    def stay(a):
        return pltpu.make_async_copy(xb.at[a, d - om * H], acts.at[a, d], a_lsem.at[a])

    def act_own(a, src):
        col = pl.multiple_of(((d - m * H) * 2 + m) * F, F)
        return pltpu.make_async_copy(src.at[:, pl.ds(col, F)], acts.at[a, d], a_lsem.at[a])

    keeps_own = (d // H) == m

    def plane_sends(go, a, src):
        @pl.loop(0, H)
        def _(j):
            @pl.when(m * H + j != d)
            def _():
                go(act_copy(a, src, j))

    def cross_sends(go, a, src):
        @pl.loop(0, H)
        def _(j):
            go(cross_copy(a, src, j))

    for a, src in ((1, cot), (0, sta)):
        cross_sends(lambda c: c.start(), a, src)

    send_up.start()
    send_down.start()
    for a, src in ((0, sta), (1, cot)):
        plane_sends(lambda c: c.start(), a, src)

        @pl.when(keeps_own)
        def _():
            act_own(a, src).start()

    g_own[...] = gain[...].astype(F32)
    gain_copy = rcopy(g_own, g_rem, g_ssem, g_rsem, peer)
    gain_copy.start()

    keep_row = jnp.logical_or(keep[...] == 1, s != 0)

    def at(i, size=C):
        return pl.ds(pl.multiple_of(i * size, size), size)

    def fold(v):
        total = v[:, :128]
        for k in range(1, v.shape[1] // 128):
            total = total + v[:, 128 * k:128 * (k + 1)]
        return total

    def squares(i, carry):
        cx, cs = carry
        v = jnp.where(keep_row, arr[:, at(i)].astype(F32), maskv[:, at(i)].astype(F32))
        xin[:, at(i)] = v.astype(BF16)
        w = sta[:, at(i)].astype(F32)
        return cx + fold(v * v), cs + fold(w * w)

    zero = jnp.zeros((rows, 128), F32)
    cx, cs = lax.fori_loop(0, chunks, squares, (zero, zero))
    lane = lax.broadcasted_iota(jnp.int32, (rows, 128), 1)
    ss_loc[...] = jnp.where(
        lane < 64, jnp.sum(cx, axis=1, keepdims=True), jnp.sum(cs, axis=1, keepdims=True)
    )
    ss_copy = rcopy(ss_loc, ss_rem, ss_ssem, ss_rsem, peer)
    ss_copy.start()

    def part_copy(k):
        return rcopy(part.at[k], part_rem.at[k], p_ssem.at[k], p_rsem.at[k], peer)

    for a in (1, 0):
        @pl.loop(0, H)
        def _(j):
            cross_copy(a, sta, j).wait_recv()

            @pl.when(om * H + j != d)
            def _():
                pass_on(a, j).start()

            @pl.when(om * H + j == d)
            def _():
                stay(a).start()

    acc0 = jnp.zeros((rows, 2 * units), F32)
    own_up.wait()
    send_up.wait_recv()
    part[0] = lax.fori_loop(
        0, chunks, lambda i, acc: acc + dot(cot[:, at(i)], wu[:, at(i)], ((1,), (1,))), acc0
    )
    part_copy(0).start()

    ss_copy.wait_recv()
    total = (ss_loc[...] + ss_rem[...]) / full
    scales = lax.rsqrt(total + 1e-05)
    scale_f = scales[:, 0:1]
    scale_b = scales[:, 127:128]
    sc_all[d] = jnp.broadcast_to(scale_b, (rows, 128))

    def sc_copy(i):
        return rcopy(sc_all.at[d], sc_all.at[d], sc_ssem.at[i], sc_rsem.at[d],
                     (lax.rem(d + i, Z), s, m))

    @pl.loop(1, Z)
    def _(i):
        sc_copy(i).start()

    def normalise(k, src, scale):
        @pl.loop(0, chunks)
        def _(i):
            normed[k, :, at(i)] = (
                src[:, at(i)].astype(F32) * scale * g_own[:, at(i)]
            ).astype(BF16)

    normalise(0, sta, scale_b)
    normalise(1, xin, scale_f)
    own_down.wait()
    send_down.wait_recv()
    for k in (0, 1):
        part[1 + k] = lax.fori_loop(
            0, chunks, lambda i, acc: acc + dot(normed[k, :, at(i)], wd[at(i), :], ((1,), (0,))), acc0
        )
        part_copy(1 + k).start()

    send_up.wait_send()
    send_down.wait_send()

    def whole_sum(k):
        part_copy(k).wait_recv()
        return jnp.concatenate(
            [part[k, :, :units] + part_rem[k, :, units:], part[k, :, units:] + part_rem[k, :, :units]],
            axis=1,
        )

    hidden_grad = whole_sum(0)
    saved_pre = whole_sum(1)
    sigma = jax.nn.sigmoid(saved_pre)
    pre_grad = (hidden_grad * sigma * (1.0 + saved_pre * (1.0 - sigma))).astype(BF16)
    pg[d, :, :2 * units] = pre_grad
    pg[d, :, 2 * units:] = (saved_pre * sigma).astype(BF16)

    def pg_copy(i):
        return rcopy(pg.at[d], pg.at[d], pg_ssem.at[i], pg_rsem.at[d],
                     (lax.rem(d + i, Z), s, m))

    @pl.loop(1, Z)
    def _(i):
        pg_copy(i).start()

    def grads(i, acc):
        v = dot(pre_grad, wd[at(i), :], ((1,), (1,))) * g_own[:, at(i)]
        scaled[:, at(i)] = v
        return acc + fold(v * sta[:, at(i)].astype(F32))

    rdot = lax.fori_loop(0, chunks, grads, zero)
    rd_loc[...] = jnp.broadcast_to(jnp.sum(rdot, axis=1, keepdims=True), (rows, 128))
    rd_copy = rcopy(rd_loc, rd_rem, rd_ssem, rd_rsem, peer)
    rd_copy.start()

    pre = whole_sum(2)
    hidden = (pre * jax.nn.sigmoid(pre)).astype(BF16)

    @pl.loop(0, chunks)
    def _(i):
        out_st[:, at(i)] = (
            xin[:, at(i)].astype(F32) + dot(hidden, wu[:, at(i)], ((1,), (0,)))
        ).astype(BF16)

    def out_copy():
        return rcopy(out_st, nxt, o_ssem.at[0], o_rsem.at[0], (d, s + 1, m))

    def grad_copy():
        return rcopy(grad_st, prv, o_ssem.at[1], o_rsem.at[1], (d, s - 1, m))

    @pl.when(s < S - 1)
    def _():
        out_copy().start()

    rd_copy.wait_recv()
    row_dot = (rd_loc[...] + rd_rem[...])[:, 0:1]
    back = scale_b * scale_b * scale_b * (row_dot / full)

    @pl.loop(0, chunks)
    def _(i):
        grad_st[:, at(i)] = (
            cot[:, at(i)].astype(F32) + scale_b * scaled[:, at(i)] - sta[:, at(i)].astype(F32) * back
        ).astype(BF16)

    @pl.when(s > 0)
    def _():
        grad_copy().start()

    @pl.when(s == 0)
    def _():
        nxt[...] = jnp.zeros_like(nxt)

    @pl.when(s == S - 1)
    def _():
        prv[...] = jnp.zeros_like(prv)

    gain_copy.wait_recv()
    FC = min(F, 512)
    slice_half = d // H
    gcol = pl.multiple_of(((d - slice_half * H) * 2 + m) * F, F)

    def wait_act(a, i):
        @pl.when(jnp.logical_and(i == d, keeps_own))
        def _():
            act_own(a, sta if a == 0 else cot).wait()

        @pl.when(jnp.logical_and(i == d, jnp.logical_not(keeps_own)))
        def _():
            stay(a).wait()

        @pl.when(i != d)
        def _():
            rcopy(acts.at[a, i], acts.at[a, i], a_ssem.at[a, 0], a_rsem.at[a, i], peer).wait_recv()

    @pl.loop(0, Z)
    def _(i):
        wait_act(1, i)

        @pl.when(i != d)
        def _():
            rcopy(pg.at[i], pg.at[i], pg_ssem.at[0], pg_rsem.at[i], peer).wait_recv()
            rcopy(sc_all.at[i], sc_all.at[i], sc_ssem.at[0], sc_rsem.at[i], peer).wait_recv()

    def res_copy(k):
        if k == 0:
            return rcopy(res_u, rem_u, r_ssem.at[0], r_rsem.at[0], peer)
        return rcopy(res_d, rem_d, r_ssem.at[1], r_rsem.at[1], peer)

    tokens = Z * rows
    hid_all = pg[:, :, 2 * units:].reshape(tokens, 2 * units)
    for c in range(F // FC):
        cols = slice(c * FC, (c + 1) * FC)
        got = dot(hid_all, acts[1, :, :, cols].reshape(tokens, FC), ((0,), (0,))) / Z
        ugo[:, pl.ds(pl.multiple_of(m * F + c * FC, FC), FC)] = got[:units]
        res_u[:, cols] = got[units:].astype(BF16)
    res_copy(0).start()

    @pl.loop(0, Z)
    def _(i):
        wait_act(0, i)
        g = jnp.where(slice_half == m, g_own[:, pl.ds(gcol, F)], g_rem[:, pl.ds(gcol, F)])
        nall[i] = (acts[0, i].astype(F32) * sc_all[i][:, 0:1] * g).astype(BF16)

    pg_all = pg[:, :, :2 * units].reshape(tokens, 2 * units)
    for c in range(F // FC):
        cols = slice(c * FC, (c + 1) * FC)
        got = dot(nall[:, :, cols].reshape(tokens, FC), pg_all, ((0,), (0,))) / Z
        dgo[pl.ds(pl.multiple_of(m * F + c * FC, FC), FC), :] = got[:, :units]
        res_d[cols, :] = got[:, units:].astype(BF16)
    res_copy(1).start()

    for a, src in ((0, sta), (1, cot)):
        plane_sends(lambda c: c.wait_send(), a, src)
        cross_sends(lambda c: c.wait_send(), a, src)

        @pl.loop(0, H)
        def _(j):
            @pl.when(om * H + j != d)
            def _():
                pass_on(a, j).wait_send()
    gain_copy.wait_send()
    ss_copy.wait_send()
    rd_copy.wait_send()
    for k in range(3):
        part_copy(k).wait_send()

    @pl.loop(1, Z)
    def _(i):
        sc_copy(i).wait_send()
        pg_copy(i).wait_send()

    @pl.when(s < S - 1)
    def _():
        out_copy().wait_send()
        grad_copy().wait_recv()

    @pl.when(s > 0)
    def _():
        out_copy().wait_recv()
        grad_copy().wait_send()

    theirs = pl.ds(pl.multiple_of(om * F, F), F)
    res_copy(0).wait()
    ugo[:, theirs] = rem_u[...].astype(F32)
    res_copy(1).wait()
    dgo[theirs, :] = rem_d[...].astype(F32)


def on_device(Z, S, arriving, keep_mask, mask_vector, stashed, cotangent, gain, down_adapter, up_adapter):
    _, rows, half = arriving.shape
    units = up_adapter.shape[1]
    F = half // Z
    full = 2 * half
    vm = pl.BlockSpec(memory_space=pltpu.VMEM)
    hbm = pl.BlockSpec(memory_space=pl.ANY)
    dma = pltpu.SemaphoreType.DMA
    vmem = pltpu.VMEM
    nxt, prv, dgo, ugo = pl.pallas_call(
        functools.partial(kernel, (Z, S, rows, half, units)),
        out_shape=(
            jax.ShapeDtypeStruct((rows, half), BF16),
            jax.ShapeDtypeStruct((rows, half), BF16),
            jax.ShapeDtypeStruct((full // Z, units), F32),
            jax.ShapeDtypeStruct((units, full // Z), F32),
        ),
        in_specs=[vm] * 6 + [hbm] * 2,
        out_specs=(vm,) * 4,
        scratch_shapes=[
            vmem((half, 2 * units), BF16),
            vmem((2 * units, half), BF16),
            vmem((rows, half), BF16),
            vmem((2, rows, half), BF16),
            vmem((rows, half), F32),
            vmem((2, Z, rows, F), BF16),
            vmem((Z, rows, 4 * units), BF16),
            vmem((Z, rows, 128), F32),
            vmem((Z, rows, F), BF16),
            vmem((rows, 128), F32),
            vmem((rows, 128), F32),
            vmem((1, half), F32),
            vmem((1, half), F32),
            vmem((3, rows, 2 * units), F32),
            vmem((3, rows, 2 * units), F32),
            vmem((rows, 128), F32),
            vmem((rows, 128), F32),
            vmem((rows, half), BF16),
            vmem((rows, half), BF16),
            vmem((F, units), BF16),
            vmem((units, F), BF16),
            vmem((F, units), BF16),
            vmem((units, F), BF16),
            vmem((2, Z // 2, rows, F), BF16),
            dma((2,)), dma((2,)), dma((2,)), dma, dma, dma, dma,
            dma((2, Z)), dma((2, Z)), dma((2,)), dma((2, Z // 2)), dma((2, Z // 2)),
            dma((3,)), dma((3,)), dma((Z,)), dma((Z,)), dma((Z,)), dma((Z,)), dma, dma,
            dma((2,)), dma((2,)), dma((2,)), dma((2,)),
        ],
        compiler_params=pltpu.CompilerParams(
            collective_id=0, has_side_effects=True, vmem_limit_bytes=56 * 1024 * 1024
        ),
    )(
        arriving[0], keep_mask[:, None], mask_vector[None], stashed[0], cotangent[0],
        gain, down_adapter[0], up_adapter[0],
    )
    return nxt[None], prv[None], dgo[None], ugo[None]


def solution(mesh):
    return jax.shard_map(
        functools.partial(on_device, mesh.shape["dp"], mesh.shape["section"]),
        mesh=mesh,
        in_specs=(
            P("section", "dp", "mp"),
            P("dp"),
            P("mp"),
            P("section", "dp", "mp"),
            P("section", "dp", "mp"),
            P("section", "mp"),
            P("section", None, "mp"),
            P("section", "mp", None),
        ),
        out_specs=(
            P("section", "dp", "mp"),
            P("section", "dp", "mp"),
            P("section", "dp", "mp"),
            P("section", "mp", "dp"),
        ),
        check_vma=False,
    )
```
